32 devices in a mesh: parts: 2 (over x), gx: 16 (over z, y, core).
Axes of the slice: x: 2, y: 2, z: 4, core: 2. Of those that a mesh axis runs over, the one named last changes fastest.
Arguments:
- positions: bfloat16 [3, 8, 32, 256, 128], P(None, None, 'gx', 'parts'), parts along dimension 3, may hold values from 0 to 1
- normals: bfloat16 [3, 8, 32, 256, 128], P(None, None, 'gx', 'parts'), parts along dimension 3, may hold values from -6 to 6
- counts: int32 [32, 256, 128], P('gx', 'parts'), parts along dimension 1, may hold values from 0 to 8
- screen: float32 [32, 256, 128], P('gx', 'parts'), parts along dimension 1, may hold values from 0.05 to 0.5
Outputs:
- solution_field: float32 [32, 256, 128], P('gx', 'parts'), parts along dimension 1
- residual: float32 [32, 256, 128], P('gx', 'parts'), parts along dimension 1
The draws below stay inside these ranges and needn't reach their ends.
There are 2 independent parts, one for each index of `parts`. The reference program is written for one: setup_inputs(seed, part) draws one part's arguments, and reference() takes and returns one part's arrays. A program takes and returns all parts, laid end to end along the dimension named above; each array names one. Nothing has to cross between parts.
All inputs are finite; a program needn't handle non-finite values.
Results may differ from the reference program's by a relative error of at most 0.0003.
Values sent between devices are 32-bit elements; how exact they have to be, the bound alone decides.
A program may use at most 64 MiB of HBM per device.

```python
import math
import jax
import jax.numpy as jnp

SLOTS = 8
ITERS = 3
NY = 128
NZ = 128
NX = 32


def touch_ends(values, stream_key, smallest, top_value):
    longest = values.shape.index(max(values.shape))
    spots = []
    for shift in (0, 1):
        where = [jax.random.randint(jax.random.fold_in(stream_key, axis), (), 0, length) for axis, length in enumerate(values.shape)]
        where[longest] = (where[longest] + shift) % values.shape[longest]
        spots.append(tuple(where))
    return values.at[spots[0]].set(smallest).at[spots[1]].set(top_value)


def block_levels(rng, dims, pieces, low, top_value):
    factor_of, own = 1.0, jax.random.fold_in(rng, 6)
    for dim, blocks in pieces:
        steps = jnp.exp(jax.random.uniform(jax.random.fold_in(own, dim), (blocks,), jnp.float32, low / len(pieces), top_value / len(pieces)))
        factor_of = factor_of * jnp.repeat(steps, dims[dim] // blocks).reshape([-1 if axis == dim else 1 for axis in range(len(dims))])
    return factor_of


def gaussian(key, dims, deviation, limit, pieces=(), dtype=jnp.bfloat16):
    array = deviation * jax.random.normal(key, dims, jnp.float32)
    if pieces:
        array = array * block_levels(key, dims, pieces, -0.22, 0.18)
    return jnp.clip(array, -limit, limit).astype(dtype)


def setup_inputs(seed: int = 0, part: int = 0) -> dict:
    key_list = jax.random.split(jax.random.key(seed), 5)
    own_keys = jax.random.split(jax.random.fold_in(key_list[4], part), 5)
    return {
        "positions": jnp.clip(1.0 * jax.random.uniform(own_keys[0], (3, SLOTS, NX, NY, NZ), jnp.float32) ** block_levels(own_keys[0], (3, SLOTS, NX, NY, NZ), ((2, 16),), -0.2, 0.2), 0.0, 1.0).astype(jnp.bfloat16),
        "normals": gaussian(own_keys[1], (3, SLOTS, NX, NY, NZ), 1.0, 6.0, ((2, 16),)),
        "counts": touch_ends(jax.random.randint(own_keys[2], (NX, NY, NZ), 0, SLOTS + 1), jax.random.fold_in(own_keys[2], 1), 0, SLOTS).astype(jnp.int32),
        "screen": jnp.clip(jnp.exp(math.log(0.5) - 2.3025851 * jax.random.uniform(own_keys[3], (NX, NY, NZ), jnp.float32) ** block_levels(own_keys[3], (NX, NY, NZ), ((0, 16),), -0.2, 0.2)), 0.05, 0.5),
    }


def spline_weights(fraction):
    return [0.5 * (1.0 - fraction) ** 2, 0.75 - (fraction - 0.5) ** 2, 0.5 * fraction * fraction]


def splat_cells(positions, normals, counts):
    slot_total = positions.shape[1]
    cells_x, cells_y, cells_z = counts.shape
    accums = [jnp.zeros((3, cells_x, cells_y, cells_z), jnp.float32) for offset_index in range(27)]
    for slot_index in range(slot_total):
        active = (counts > slot_index).astype(jnp.float32)
        vectors = normals[:, slot_index].astype(jnp.float32) * active
        fraction = positions[:, slot_index].astype(jnp.float32)
        along_x = spline_weights(fraction[0])
        along_y = spline_weights(fraction[1])
        along_z = spline_weights(fraction[2])
        for first_off in range(3):
            for second_off in range(3):
                planar = along_x[first_off] * along_y[second_off]
                for third_off in range(3):
                    place = first_off * 9 + second_off * 3 + third_off
                    accums[place] = accums[place] + vectors * (planar * along_z[third_off])
    padded = jnp.zeros((3, cells_x + 2, cells_y + 2, cells_z + 2), jnp.float32)
    for first_off in range(3):
        for second_off in range(3):
            for third_off in range(3):
                place = first_off * 9 + second_off * 3 + third_off
                padded = padded + jnp.pad(accums[place], ((0, 0), (first_off, 2 - first_off), (second_off, 2 - second_off), (third_off, 2 - third_off)))
    return padded


def divergence(ghost_x, field):
    deriv_x = 0.5 * (ghost_x[2:] - ghost_x[:-2])
    padded_y = jnp.pad(field[1], ((0, 0), (1, 1), (0, 0)))
    deriv_y = 0.5 * (padded_y[:, 2:] - padded_y[:, :-2])
    padded_z = jnp.pad(field[2], ((0, 0), (0, 0), (1, 1)))
    deriv_z = 0.5 * (padded_z[:, :, 2:] - padded_z[:, :, :-2])
    return deriv_x + deriv_y + deriv_z


def stencil(padded, field, screen):
    cells_x, cells_y, cells_z = field.shape
    table = {1: 1.0, 2: 0.5, 3: 0.25}
    total = jnp.zeros_like(field)
    for offset_x in range(3):
        for offset_y in range(3):
            for offset_z in range(3):
                moved = abs(offset_x - 1) + abs(offset_y - 1) + abs(offset_z - 1)
                if moved > 0:
                    total = total + table[moved] * padded[offset_x:offset_x + cells_x, offset_y:offset_y + cells_y, offset_z:offset_z + cells_z]
    return screen * field + 0.25 * (14.0 * field - total)


def reference(positions, normals, counts, screen):
    padded = splat_cells(positions, normals, counts)
    field = padded[:, 1:-1, 1:-1, 1:-1]
    ghost_x = jnp.pad(field[0], ((1, 1), (0, 0), (0, 0)))
    right_side = divergence(ghost_x, field)
    solution_field = jnp.zeros_like(right_side)
    residual, direction = right_side, right_side
    norm_now = jnp.sum(residual * residual)
    for step_index in range(ITERS):
        image = stencil(jnp.pad(direction, 1), direction, screen)
        alpha = norm_now / jnp.sum(direction * image)
        solution_field = solution_field + alpha * direction
        residual = residual - alpha * image
        norm_next = jnp.sum(residual * residual)
        direction = residual + (norm_next / norm_now) * direction
        norm_now = norm_next
    return solution_field, residual
```

```python
import functools

import jax
import jax.numpy as jnp
from jax import lax
from jax.experimental import pallas as pl
from jax.experimental.pallas import tpu as pltpu
from jax.sharding import PartitionSpec as P

ITERS = 3
SHIFT = 2.25
CHUNK = 32
MESH = pl.DeviceIdType.MESH


def lane_before(a):
    lane = lax.broadcasted_iota(jnp.int32, a.shape, 1)
    return jnp.where(lane == 0, 0.0, pltpu.roll(a, 1, 1))


def lane_after(a):
    lane = lax.broadcasted_iota(jnp.int32, a.shape, 1)
    size = a.shape[1]
    return jnp.where(lane == size - 1, 0.0, pltpu.roll(a, size - 1, 1))


def row_before(a):
    row = lax.broadcasted_iota(jnp.int32, a.shape, 0)
    return jnp.where(row == 0, 0.0, pltpu.roll(a, 1, 0))


def row_after(a):
    row = lax.broadcasted_iota(jnp.int32, a.shape, 0)
    size = a.shape[0]
    return jnp.where(row == size - 1, 0.0, pltpu.roll(a, size - 1, 0))


def taps(m0, m1, m2):
    twice = m1 + m1
    return (m0 - twice) + m2, (m0 + twice) - (m2 + m2), m2


def gather_moments(pos, nrm, cnt, c, rows, half, plane, slots):
    part = slice(8 * half, 8 * half + 8)
    live = cnt[plane, rows, :][part]
    sums = [None] * 27
    for s in range(slots):
        n = nrm[c, s, plane, rows, :].astype(jnp.float32)[part]
        x = pos[0, s, plane, rows, :].astype(jnp.float32)[part]
        y = pos[1, s, plane, rows, :].astype(jnp.float32)[part]
        z = pos[2, s, plane, rows, :].astype(jnp.float32)[part]
        tx = jnp.where(live > s, n, 0.0)
        for p in range(3):
            if p:
                tx = tx * x
            ty = tx
            for q in range(3):
                if q:
                    ty = ty * y
                tz = ty
                for r in range(3):
                    if r:
                        tz = tz * z
                    at = 9 * p + 3 * q + r
                    sums[at] = tz if sums[at] is None else sums[at] + tz
    return sums


def kernel(n, slots, pos_hbm, nrm_hbm, cnt_hbm, scr_hbm, sol_ref, res_ref,
           pos, nrm, cnt, scr, g, out_l, out_r, in_l, in_r, v, halo, part, parts,
           load_sem, send_sem, recv_sem, psend, precv):
    me = lax.axis_index("gx")
    my_part = lax.axis_index("parts")
    ny = cnt.shape[1]
    chunks = ny // CHUNK
    has_left, has_right = me > 0, me < n - 1

    def peer(i):
        return {"parts": my_part, "gx": i}

    def loads(k):
        rows = pl.ds(pl.multiple_of(k * CHUNK, CHUNK), CHUNK)
        return (
            pltpu.make_async_copy(pos_hbm.at[:, :, :, rows, :], pos.at[:, :, :, rows, :], load_sem.at[0, k]),
            pltpu.make_async_copy(nrm_hbm.at[:, :, :, rows, :], nrm.at[:, :, :, rows, :], load_sem.at[1, k]),
            pltpu.make_async_copy(cnt_hbm.at[:, rows, :], cnt.at[:, rows, :], load_sem.at[2, k]),
        )

    for k in range(chunks):
        for copy in loads(k):
            copy.start()
    scr_copy = pltpu.make_async_copy(scr_hbm, scr, load_sem.at[3, 0])
    scr_copy.start()

    barrier = pltpu.get_barrier_semaphore()

    @pl.loop(1, n)
    def _(d):
        pl.semaphore_signal(barrier, inc=1, device_id=peer(lax.rem(me + d, n)), device_id_type=MESH)

    @pl.loop(0, chunks)
    def _(k):
        for copy in loads(k):
            copy.wait()

        @pl.loop(0, CHUNK // 16)
        def _(j):
            start = pl.multiple_of(k * CHUNK + j * 16, 16)
            rows = pl.ds(start, 16)

            @pl.loop(0, 3)
            def _(c):
                for half in range(2):
                    low = gather_moments(pos, nrm, cnt, c, rows, half, 0, slots)
                    high = gather_moments(pos, nrm, cnt, c, rows, half, 1, slots)
                    own = pl.ds(pl.multiple_of(start + 8 * half, 8), 8)
                    for q in range(3):
                        planes = [[], [], [], []]
                        for r in range(3):
                            at = 3 * q + r
                            a = taps(low[at], low[9 + at], low[18 + at])
                            b = taps(high[at], high[9 + at], high[18 + at])
                            planes[0].append(a[0])
                            planes[1].append(a[1] + b[0])
                            planes[2].append(a[2] + b[1])
                            planes[3].append(b[2])
                        for i in range(4):
                            t = taps(*planes[i])
                            g[c, i, q, own, :] = lane_after(t[0]) + t[1] + lane_before(t[2])

    def along_y(c, i):
        t = taps(g[c, i, 0], g[c, i, 1], g[c, i, 2])
        return row_after(t[0]) + t[1] + row_before(t[2])

    def across(i):
        fy = along_y(1, i)
        fz = along_y(2, i)
        return (row_after(fy) - row_before(fy)) + (lane_after(fz) - lane_before(fz))

    scale = 1.0 / 16.0
    for i in range(4):
        v[i // 2, i % 2] = along_y(0, i)
    out_l[0] = scale * v[0, 0]
    out_l[1] = scale * (v[0, 1] + across(0))
    out_r[0] = scale * (across(3) - v[1, 0])
    out_r[1] = -scale * v[1, 1]

    pl.semaphore_wait(barrier, n - 1)

    def to_left(src, dst, at):
        return pltpu.make_async_remote_copy(
            src_ref=src, dst_ref=dst, send_sem=send_sem.at[0, at], recv_sem=recv_sem.at[0, at],
            device_id=peer(jnp.maximum(me - 1, 0)), device_id_type=MESH)

    def to_right(src, dst, at):
        return pltpu.make_async_remote_copy(
            src_ref=src, dst_ref=dst, send_sem=send_sem.at[1, at], recv_sem=recv_sem.at[1, at],
            device_id=peer(jnp.minimum(me + 1, n - 1)), device_id_type=MESH)

    pairs = [(to_left(out_l, in_r, 0), to_right(out_r, in_l, 0))]
    for k in range(3):
        pairs.append((to_left(v.at[k, 0], halo.at[k, 1], k + 1),
                      to_right(v.at[k, 1], halo.at[k, 0], k + 1)))

    def begin(at):
        @pl.when(has_left)
        def _():
            pairs[at][0].start()

        @pl.when(has_right)
        def _():
            pairs[at][1].start()

    def arrive(at):
        @pl.when(has_right)
        def _():
            pairs[at][0].wait_recv()

        @pl.when(has_left)
        def _():
            pairs[at][1].wait_recv()

    begin(0)
    inner0 = across(1) + v[1, 0] - jnp.where(has_left, v[0, 0], 0.0)
    inner1 = across(2) + jnp.where(has_right, v[1, 1], 0.0) - v[0, 1]
    v[0, 0] = scale * inner0
    v[0, 1] = scale * inner1
    @pl.when(jnp.logical_not(has_left))
    def _():
        in_l[...] = jnp.zeros_like(in_l)
        for k in range(3):
            halo[k, 0] = jnp.zeros_like(halo[k, 0])

    @pl.when(jnp.logical_not(has_right))
    def _():
        in_r[...] = jnp.zeros_like(in_r)
        for k in range(3):
            halo[k, 1] = jnp.zeros_like(halo[k, 1])

    scr_copy.wait()
    arrive(0)
    v[0, 0] = v[0, 0] + (in_l[0] + in_r[0])
    v[0, 1] = v[0, 1] + (in_l[1] + in_r[1])

    def smooth(a, b, c):
        u = a + (b + b) + c
        u = row_before(u) + (u + u) + row_after(u)
        return lane_before(u) + (u + u) + lane_after(u)

    def fold(a):
        return jnp.sum(a, axis=0, keepdims=True)

    def dot(i, j):
        return fold(v[i, 0] * v[j, 0] + v[i, 1] * v[j, 1])

    for k in range(3):
        begin(k + 1)
        part[2 * k:2 * k + 1, :] = dot(k, k)
        if k:
            part[2 * k - 1:2 * k, :] = dot(k - 1, k)
        arrive(k + 1)
        a, b = v[k, 0], v[k, 1]
        v[k + 1, 0] = (scr[0] + (4.0 - SHIFT)) * a - scale * smooth(halo[k, 0], a, b)
        v[k + 1, 1] = (scr[1] + (4.0 - SHIFT)) * b - scale * smooth(a, b, halo[k, 1])
    part[5:6, :] = dot(2, 3)
    part[6:8, :] = jnp.zeros((2, part.shape[1]), jnp.float32)

    def spread(d):
        return pltpu.make_async_remote_copy(
            src_ref=part, dst_ref=parts.at[d], send_sem=psend.at[d], recv_sem=precv.at[d],
            device_id=peer(lax.rem(me + d, n)), device_id_type=MESH)

    @pl.loop(1, n)
    def _(d):
        spread(d).start()

    @pl.loop(1, n)
    def _(d):
        spread(d).wait_recv()

    def order(d, total):
        return total + parts[d]

    parts[0] = part[...]
    total = lax.fori_loop(0, n, order, jnp.zeros(part.shape, jnp.float32))
    total = jnp.sum(total, axis=1, keepdims=True)
    moment = [jnp.broadcast_to(total[k:k + 1, :], (8, 128)) for k in range(6)]

    def inner(a, b):
        terms = {}
        for i, s in enumerate(a):
            for j, t in enumerate(b):
                terms[i + j] = s * t if i + j not in terms else terms[i + j] + s * t
        out = None
        for k, s in terms.items():
            out = s * moment[k] if out is None else out + s * moment[k]
        return out

    one = jnp.ones((8, 128), jnp.float32)
    none = jnp.zeros((8, 128), jnp.float32)
    sol, res, way, rr = [], [one], [one], moment[0]
    for step in range(ITERS):
        image = [SHIFT * s for s in way] + [none]
        image = [image[k] + (way[k - 1] if k else none) for k in range(len(image))]
        alpha = rr / inner(way, image)
        sol = [(sol[k] if k < len(sol) else none) + alpha * s for k, s in enumerate(way)]
        res = [(res[k] if k < len(res) else none) - alpha * s for k, s in enumerate(image)]
        if step < ITERS - 1:
            new = inner(res, res)
            beta = new / rr
            way = [s + (beta * way[k] if k < len(way) else none) for k, s in enumerate(res)]
            rr = new

    sol = [s[0:1, :] for s in sol]
    res = [s[0:1, :] for s in res]
    for i in range(2):
        sol_ref[i] = sol[0] * v[0, i] + sol[1] * v[1, i] + sol[2] * v[2, i]
        res_ref[i] = res[0] * v[0, i] + res[1] * v[1, i] + res[2] * v[2, i] + res[3] * v[3, i]

    @pl.loop(1, n)
    def _(d):
        spread(d).wait_send()

    @pl.when(has_left)
    def _():
        for pair in pairs:
            pair[0].wait_send()

    @pl.when(has_right)
    def _():
        for pair in pairs:
            pair[1].wait_send()


def local(n, positions, normals, counts, screen):
    slots = positions.shape[1]
    plane = counts.shape[1:]
    chunks = plane[0] // CHUNK
    f32 = jnp.float32
    out = jax.ShapeDtypeStruct(counts.shape, f32)
    return tuple(pl.pallas_call(
        functools.partial(kernel, n, slots),
        out_shape=(out, out),
        in_specs=[pl.BlockSpec(memory_space=pl.ANY)] * 4,
        out_specs=(pl.BlockSpec(memory_space=pltpu.VMEM),) * 2,
        scratch_shapes=[
            pltpu.VMEM(positions.shape, positions.dtype),
            pltpu.VMEM(normals.shape, normals.dtype),
            pltpu.VMEM(counts.shape, counts.dtype),
            pltpu.VMEM(screen.shape, f32),
            pltpu.VMEM((3, 4, 3) + plane, f32),
            pltpu.VMEM((2,) + plane, f32),
            pltpu.VMEM((2,) + plane, f32),
            pltpu.VMEM((2,) + plane, f32),
            pltpu.VMEM((2,) + plane, f32),
            pltpu.VMEM((4, 2) + plane, f32),
            pltpu.VMEM((3, 2) + plane, f32),
            pltpu.VMEM((8, 128), f32),
            pltpu.VMEM((n, 8, 128), f32),
            pltpu.SemaphoreType.DMA((4, chunks)),
            pltpu.SemaphoreType.DMA((2, 4)),
            pltpu.SemaphoreType.DMA((2, 4)),
            pltpu.SemaphoreType.DMA((n,)),
            pltpu.SemaphoreType.DMA((n,)),
        ],
        compiler_params=pltpu.CompilerParams(
            collective_id=0, has_side_effects=True, vmem_limit_bytes=32 * 1024 * 1024
        ),
    )(positions, normals, counts, screen))


def solution(mesh):
    placed = (
        P(None, None, "gx", "parts", None),
        P(None, None, "gx", "parts", None),
        P("gx", "parts", None),
        P("gx", "parts", None),
    )
    return jax.shard_map(
        functools.partial(local, mesh.shape["gx"]),
        mesh=mesh,
        in_specs=placed,
        out_specs=(P("gx", "parts", None), P("gx", "parts", None)),
        check_vma=False,
    )
```

```python
import functools

import jax
import jax.numpy as jnp
from jax import lax
from jax.experimental import pallas as pl
from jax.experimental.pallas import tpu as pltpu
from jax.sharding import PartitionSpec as P

ITERS = 3
SHIFT = 2.25
CHUNK = 32
MESH = pl.DeviceIdType.MESH


def lane_before(a):
    lane = lax.broadcasted_iota(jnp.int32, a.shape, 1)
    return jnp.where(lane == 0, 0.0, pltpu.roll(a, 1, 1))


def lane_after(a):
    lane = lax.broadcasted_iota(jnp.int32, a.shape, 1)
    size = a.shape[1]
    return jnp.where(lane == size - 1, 0.0, pltpu.roll(a, size - 1, 1))


def row_before(a):
    row = lax.broadcasted_iota(jnp.int32, a.shape, 0)
    return jnp.where(row == 0, 0.0, pltpu.roll(a, 1, 0))


def row_after(a):
    row = lax.broadcasted_iota(jnp.int32, a.shape, 0)
    size = a.shape[0]
    return jnp.where(row == size - 1, 0.0, pltpu.roll(a, size - 1, 0))


def taps(m0, m1, m2):
    twice = m1 + m1
    return (m0 - twice) + m2, (m0 + twice) - (m2 + m2), m2


def gather_moments(pos, nrm, cnt, c, rows, half, plane, slots):
    part = slice(8 * half, 8 * half + 8)
    live = cnt[plane, rows, :][part]
    sums = [None] * 27
    for s in range(slots):
        n = nrm[c, s, plane, rows, :].astype(jnp.float32)[part]
        x = pos[0, s, plane, rows, :].astype(jnp.float32)[part]
        y = pos[1, s, plane, rows, :].astype(jnp.float32)[part]
        z = pos[2, s, plane, rows, :].astype(jnp.float32)[part]
        tx = jnp.where(live > s, n, 0.0)
        for p in range(3):
            if p:
                tx = tx * x
            ty = tx
            for q in range(3):
                if q:
                    ty = ty * y
                tz = ty
                for r in range(3):
                    if r:
                        tz = tz * z
                    at = 9 * p + 3 * q + r
                    sums[at] = tz if sums[at] is None else sums[at] + tz
    return sums


def kernel(n, slots, pos_hbm, nrm_hbm, cnt_hbm, scr_hbm, sol_ref, res_ref,
           pos, nrm, cnt, scr, g, f0, out_l, out_r, in_l, in_r, v0, v1, v2, v3, part, parts,
           load_sem, send_sem, recv_sem, psend, precv):
    me = lax.axis_index("gx")
    my_part = lax.axis_index("parts")
    ny = cnt.shape[1]
    chunks = ny // CHUNK
    has_left, has_right = me > 0, me < n - 1

    def peer(i):
        return {"parts": my_part, "gx": i}

    def loads(k):
        rows = pl.ds(pl.multiple_of(k * CHUNK, CHUNK), CHUNK)
        return (
            pltpu.make_async_copy(pos_hbm.at[:, :, :, rows, :], pos.at[:, :, :, rows, :], load_sem.at[0, k]),
            pltpu.make_async_copy(nrm_hbm.at[:, :, :, rows, :], nrm.at[:, :, :, rows, :], load_sem.at[1, k]),
            pltpu.make_async_copy(cnt_hbm.at[:, rows, :], cnt.at[:, rows, :], load_sem.at[2, k]),
        )

    for k in range(chunks):
        for copy in loads(k):
            copy.start()
    scr_copy = pltpu.make_async_copy(scr_hbm, scr.at[2:4], load_sem.at[3, 0])
    scr_copy.start()

    barrier = pltpu.get_barrier_semaphore()

    @pl.loop(1, n)
    def _(d):
        pl.semaphore_signal(barrier, inc=1, device_id=peer(lax.rem(me + d, n)), device_id_type=MESH)

    def ship(src, dst, by, at):
        copy = pltpu.make_async_remote_copy(
            src_ref=src, dst_ref=dst, send_sem=send_sem.at[at], recv_sem=recv_sem.at[at],
            device_id=peer(jnp.clip(me + by, 0, n - 1)), device_id_type=MESH)
        to, source = me + by, me - by
        return copy, (to >= 0) & (to < n), (source >= 0) & (source < n)

    ships = {
        "screen": (ship(scr.at[2:4], scr.at[4:6], -1, 0), ship(scr.at[2:4], scr.at[0:2], 1, 1)),
        "rim": (ship(out_l, in_r, -1, 2), ship(out_r, in_l, 1, 3)),
        "first": (ship(v0.at[3], v0.at[5], -1, 4), ship(v0.at[4], v0.at[2], 1, 5)),
        "second": (ship(v0.at[4], v0.at[6], -1, 6), ship(v0.at[3], v0.at[1], 1, 7)),
        "third": (ship(v0.at[3], v0.at[7], -2, 8), ship(v0.at[4], v0.at[0], 2, 9)),
    }

    def begin(name):
        for copy, sends, _ in ships[name]:
            pl.when(sends)(copy.start)

    def arrive(name):
        for copy, _, receives in ships[name]:
            pl.when(receives)(copy.wait_recv)

    def sent(name):
        for copy, sends, _ in ships[name]:
            pl.when(sends)(copy.wait_send)

    @pl.when(jnp.logical_not(has_left))
    def _():
        in_l[...] = jnp.zeros_like(in_l)
        v0[1:3] = jnp.zeros_like(v0[1:3])
        scr[0:2] = jnp.zeros_like(scr[0:2])

    @pl.when(jnp.logical_not(has_right))
    def _():
        in_r[...] = jnp.zeros_like(in_r)
        v0[5:7] = jnp.zeros_like(v0[5:7])
        scr[4:6] = jnp.zeros_like(scr[4:6])

    @pl.when(me < 2)
    def _():
        v0[0] = jnp.zeros_like(v0[0])

    @pl.when(me >= n - 2)
    def _():
        v0[7] = jnp.zeros_like(v0[7])

    @pl.loop(0, chunks)
    def _(k):
        for copy in loads(k):
            copy.wait()

        @pl.when(k == chunks - 1)
        def _():
            scr_copy.wait()
            pl.semaphore_wait(barrier, n - 1)
            begin("screen")

        @pl.loop(0, CHUNK // 16)
        def _(j):
            start = pl.multiple_of(k * CHUNK + j * 16, 16)
            rows = pl.ds(start, 16)

            @pl.loop(0, 3)
            def _(c):
                for half in range(2):
                    low = gather_moments(pos, nrm, cnt, c, rows, half, 0, slots)
                    high = gather_moments(pos, nrm, cnt, c, rows, half, 1, slots)
                    own = pl.ds(pl.multiple_of(start + 8 * half, 8), 8)
                    for q in range(3):
                        planes = [[], [], [], []]
                        for r in range(3):
                            at = 3 * q + r
                            a = taps(low[at], low[9 + at], low[18 + at])
                            b = taps(high[at], high[9 + at], high[18 + at])
                            planes[0].append(a[0])
                            planes[1].append(a[1] + b[0])
                            planes[2].append(a[2] + b[1])
                            planes[3].append(b[2])
                        for i in range(4):
                            t = taps(*planes[i])
                            g[c, i, q, own, :] = lane_after(t[0]) + t[1] + lane_before(t[2])

    def along_y(c, i):
        t = taps(g[c, i, 0], g[c, i, 1], g[c, i, 2])
        return row_after(t[0]) + t[1] + row_before(t[2])

    def across(i):
        fy = along_y(1, i)
        fz = along_y(2, i)
        return (row_after(fy) - row_before(fy)) + (lane_after(fz) - lane_before(fz))

    scale = 1.0 / 16.0
    for i in range(4):
        f0[i] = along_y(0, i)
    out_l[0] = scale * f0[0]
    out_l[1] = scale * (f0[1] + across(0))
    out_r[0] = scale * (across(3) - f0[2])
    out_r[1] = -scale * f0[3]
    begin("rim")
    inner0 = scale * (across(1) + f0[2] - jnp.where(has_left, f0[0], 0.0))
    v0[3] = inner0
    inner1 = scale * (across(2) + jnp.where(has_right, f0[3], 0.0) - f0[1])
    v0[4] = inner1
    arrive("rim")
    v0[3] = v0[3] + (in_l[0] + in_r[0])
    v0[4] = v0[4] + (in_l[1] + in_r[1])
    for name in ("first", "second", "third"):
        begin(name)

    def smooth(a):
        a = row_before(a) + (a + a) + row_after(a)
        return lane_before(a) + (a + a) + lane_after(a)

    def apply(src, dst, smoothed, i, lo):
        u = smoothed[i] + (smoothed[i + 1] + smoothed[i + 1]) + smoothed[i + 2]
        out = (scr[lo + i] + (4.0 - SHIFT)) * src[i + 1] - scale * u
        if lo + i < 2:
            out = jnp.where(has_left, out, 0.0)
        if lo + i > 3:
            out = jnp.where(has_right, out, 0.0)
        dst[i] = out

    def dot(a, i, b, j):
        return jnp.sum(a[i] * b[j] + a[i + 1] * b[j + 1], axis=0, keepdims=True)

    def smooth_into(dst, src, planes):
        for i in planes:
            dst[i] = smooth(src[i])

    s0 = [g.at[0, i // 3, i % 3] for i in range(8)]
    s1 = [g.at[1, i // 3, i % 3] for i in range(6)]
    s2 = [g.at[2, i // 3, i % 3] for i in range(4)]

    class Planes:
        def __init__(self, refs):
            self.refs = refs

        def __getitem__(self, i):
            return self.refs[i][...]

        def __setitem__(self, i, value):
            self.refs[i][...] = value

    s0, s1, s2 = Planes(s0), Planes(s1), Planes(s2)
    smooth_into(s0, v0, (3, 4))
    part[0:1, :] = dot(v0, 3, v0, 3)
    arrive("screen")
    arrive("first")
    smooth_into(s0, v0, (2, 5))
    for i in (2, 3):
        apply(v0, v1, s0, i, 0)
    part[1:2, :] = dot(v0, 3, v1, 2)
    part[2:3, :] = dot(v1, 2, v1, 2)
    smooth_into(s1, v1, (2, 3))
    arrive("second")
    smooth_into(s0, v0, (1, 6))
    for i in (1, 4):
        apply(v0, v1, s0, i, 0)
    smooth_into(s1, v1, (1, 4))
    for i in (1, 2):
        apply(v1, v2, s1, i, 1)
    part[3:4, :] = dot(v1, 2, v2, 1)
    part[4:5, :] = dot(v2, 1, v2, 1)
    smooth_into(s2, v2, (1, 2))
    arrive("third")
    smooth_into(s0, v0, (0, 7))
    for i in (0, 5):
        apply(v0, v1, s0, i, 0)
    smooth_into(s1, v1, (0, 5))
    for i in (0, 3):
        apply(v1, v2, s1, i, 1)
    smooth_into(s2, v2, (0, 3))
    for i in (0, 1):
        apply(v2, v3, s2, i, 2)
    part[5:6, :] = dot(v2, 1, v3, 0)
    part[6:8, :] = jnp.zeros((2, part.shape[1]), jnp.float32)

    def spread(d):
        return pltpu.make_async_remote_copy(
            src_ref=part, dst_ref=parts.at[d], send_sem=psend.at[d], recv_sem=precv.at[d],
            device_id=peer(lax.rem(me + d, n)), device_id_type=MESH)

    @pl.loop(1, n)
    def _(d):
        spread(d).start()

    @pl.loop(1, n)
    def _(d):
        spread(d).wait_recv()

    def order(d, total):
        return total + parts[d]

    parts[0] = part[...]
    total = lax.fori_loop(0, n, order, jnp.zeros(part.shape, jnp.float32))
    total = jnp.sum(total, axis=1, keepdims=True)
    moment = [jnp.broadcast_to(total[k:k + 1, :], (8, 128)) for k in range(6)]

    def inner(a, b):
        terms = {}
        for i, s in enumerate(a):
            for j, t in enumerate(b):
                terms[i + j] = s * t if i + j not in terms else terms[i + j] + s * t
        out = None
        for k, s in terms.items():
            out = s * moment[k] if out is None else out + s * moment[k]
        return out

    one = jnp.ones((8, 128), jnp.float32)
    none = jnp.zeros((8, 128), jnp.float32)
    sol, res, way, rr = [], [one], [one], moment[0]
    for step in range(ITERS):
        image = [SHIFT * s for s in way] + [none]
        image = [image[k] + (way[k - 1] if k else none) for k in range(len(image))]
        alpha = rr / inner(way, image)
        sol = [(sol[k] if k < len(sol) else none) + alpha * s for k, s in enumerate(way)]
        res = [(res[k] if k < len(res) else none) - alpha * s for k, s in enumerate(image)]
        if step < ITERS - 1:
            new = inner(res, res)
            beta = new / rr
            way = [s + (beta * way[k] if k < len(way) else none) for k, s in enumerate(res)]
            rr = new

    sol = [s[0:1, :] for s in sol]
    res = [s[0:1, :] for s in res]
    for i in range(2):
        sol_ref[i] = sol[0] * v0[3 + i] + sol[1] * v1[2 + i] + sol[2] * v2[1 + i]
        res_ref[i] = res[0] * v0[3 + i] + res[1] * v1[2 + i] + res[2] * v2[1 + i] + res[3] * v3[i]

    @pl.loop(1, n)
    def _(d):
        spread(d).wait_send()

    for name in ships:
        sent(name)


def local(n, positions, normals, counts, screen):
    slots = positions.shape[1]
    plane = counts.shape[1:]
    chunks = plane[0] // CHUNK
    f32 = jnp.float32
    out = jax.ShapeDtypeStruct(counts.shape, f32)
    return tuple(pl.pallas_call(
        functools.partial(kernel, n, slots),
        out_shape=(out, out),
        in_specs=[pl.BlockSpec(memory_space=pl.ANY)] * 4,
        out_specs=(pl.BlockSpec(memory_space=pltpu.VMEM),) * 2,
        scratch_shapes=[
            pltpu.VMEM(positions.shape, positions.dtype),
            pltpu.VMEM(normals.shape, normals.dtype),
            pltpu.VMEM(counts.shape, counts.dtype),
            pltpu.VMEM((6,) + plane, f32),
            pltpu.VMEM((3, 4, 3) + plane, f32),
            pltpu.VMEM((4,) + plane, f32),
            pltpu.VMEM((2,) + plane, f32),
            pltpu.VMEM((2,) + plane, f32),
            pltpu.VMEM((2,) + plane, f32),
            pltpu.VMEM((2,) + plane, f32),
            pltpu.VMEM((8,) + plane, f32),
            pltpu.VMEM((6,) + plane, f32),
            pltpu.VMEM((4,) + plane, f32),
            pltpu.VMEM((2,) + plane, f32),
            pltpu.VMEM((8, 128), f32),
            pltpu.VMEM((n, 8, 128), f32),
            pltpu.SemaphoreType.DMA((4, chunks)),
            pltpu.SemaphoreType.DMA((10,)),
            pltpu.SemaphoreType.DMA((10,)),
            pltpu.SemaphoreType.DMA((n,)),
            pltpu.SemaphoreType.DMA((n,)),
        ],
        compiler_params=pltpu.CompilerParams(
            collective_id=0, has_side_effects=True, vmem_limit_bytes=60 * 1024 * 1024
        ),
    )(positions, normals, counts, screen))


def solution(mesh):
    placed = (
        P(None, None, "gx", "parts", None),
        P(None, None, "gx", "parts", None),
        P("gx", "parts", None),
        P("gx", "parts", None),
    )
    return jax.shard_map(
        functools.partial(local, mesh.shape["gx"]),
        mesh=mesh,
        in_specs=placed,
        out_specs=(P("gx", "parts", None), P("gx", "parts", None)),
        check_vma=False,
    )
```

```python
import functools

import jax
import jax.numpy as jnp
from jax import lax
from jax.experimental import pallas as pl
from jax.experimental.pallas import tpu as pltpu
from jax.sharding import PartitionSpec as P

ITERS = 3
SHIFT = 2.25
CHUNK = 32
MESH = pl.DeviceIdType.MESH


def lane_before(a):
    lane = lax.broadcasted_iota(jnp.int32, a.shape, 1)
    return jnp.where(lane == 0, 0.0, pltpu.roll(a, 1, 1))


def lane_after(a):
    lane = lax.broadcasted_iota(jnp.int32, a.shape, 1)
    size = a.shape[1]
    return jnp.where(lane == size - 1, 0.0, pltpu.roll(a, size - 1, 1))


def row_before(a):
    row = lax.broadcasted_iota(jnp.int32, a.shape, 0)
    return jnp.where(row == 0, 0.0, pltpu.roll(a, 1, 0))


def row_after(a):
    row = lax.broadcasted_iota(jnp.int32, a.shape, 0)
    size = a.shape[0]
    return jnp.where(row == size - 1, 0.0, pltpu.roll(a, size - 1, 0))


def taps(m0, m1, m2):
    last = m1 - m2
    return (m0 - m1) - m2, m0 + (m2 + m2), last


def gather_moments(pos, nrm, cnt, c, rows, half, plane, slots):
    part = slice(8 * half, 8 * half + 8)
    live = cnt[plane, rows, :][part]
    sums = [None] * 27
    for s in range(slots):
        n = nrm[c, s, plane, rows, :].astype(jnp.float32)[part]
        x = pos[0, s, plane, rows, :].astype(jnp.float32)[part]
        y = pos[1, s, plane, rows, :].astype(jnp.float32)[part]
        z = pos[2, s, plane, rows, :].astype(jnp.float32)[part]
        tx = jnp.where(live > s, n, 0.0)
        for p in range(3):
            if p:
                tx = tx * (x if p == 1 else 1.0 - x)
            ty = tx
            for q in range(3):
                if q:
                    ty = ty * (y if q == 1 else 1.0 - y)
                tz = ty
                for r in range(3):
                    if r:
                        tz = tz * (z if r == 1 else 1.0 - z)
                    at = 9 * p + 3 * q + r
                    sums[at] = tz if sums[at] is None else sums[at] + tz
    return sums


def kernel(n, slots, pos_hbm, nrm_hbm, cnt_hbm, scr_hbm, sol_ref, res_ref,
           pos, nrm, cnt, scr, g, f0, out_l, out_r, in_l, in_r, v0, v1, v2, v3, part, parts,
           load_sem, send_sem, recv_sem, psend, precv):
    me = lax.axis_index("gx")
    my_part = lax.axis_index("parts")
    ny = cnt.shape[1]
    chunks = ny // CHUNK
    has_left, has_right = me > 0, me < n - 1

    def peer(i):
        return {"parts": my_part, "gx": i}

    def loads(k):
        rows = pl.ds(pl.multiple_of(k * CHUNK, CHUNK), CHUNK)
        return (
            pltpu.make_async_copy(pos_hbm.at[:, :, :, rows, :], pos.at[:, :, :, rows, :], load_sem.at[0, k]),
            pltpu.make_async_copy(nrm_hbm.at[:, :, :, rows, :], nrm.at[:, :, :, rows, :], load_sem.at[1, k]),
            pltpu.make_async_copy(cnt_hbm.at[:, rows, :], cnt.at[:, rows, :], load_sem.at[2, k]),
        )

    for k in range(chunks):
        for copy in loads(k):
            copy.start()
    scr_copy = pltpu.make_async_copy(scr_hbm, scr.at[2:4], load_sem.at[3, 0])
    scr_copy.start()

    barrier = pltpu.get_barrier_semaphore()

    @pl.loop(1, n)
    def _(d):
        pl.semaphore_signal(barrier, inc=1, device_id=peer(lax.rem(me + d, n)), device_id_type=MESH)

    def ship(src, dst, by, at):
        copy = pltpu.make_async_remote_copy(
            src_ref=src, dst_ref=dst, send_sem=send_sem.at[at], recv_sem=recv_sem.at[at],
            device_id=peer(jnp.clip(me + by, 0, n - 1)), device_id_type=MESH)
        to, source = me + by, me - by
        return copy, (to >= 0) & (to < n), (source >= 0) & (source < n)

    ships = {
        "screen": (ship(scr.at[2:4], scr.at[4:6], -1, 0), ship(scr.at[2:4], scr.at[0:2], 1, 1)),
        "outer": (ship(out_l.at[0], in_r.at[0], -1, 2), ship(out_r.at[1], in_l.at[1], 1, 3)),
        "inner": (ship(out_l.at[1], in_r.at[1], -1, 10), ship(out_r.at[0], in_l.at[0], 1, 11)),
        "first": (ship(v0.at[3], v0.at[5], -1, 4), ship(v0.at[4], v0.at[2], 1, 5)),
        "second": (ship(v0.at[4], v0.at[6], -1, 6), ship(v0.at[3], v0.at[1], 1, 7)),
        "third": (ship(v0.at[3], v0.at[7], -2, 8), ship(v0.at[4], v0.at[0], 2, 9)),
    }

    def begin(name):
        for copy, sends, _ in ships[name]:
            pl.when(sends)(copy.start)

    def arrive(name):
        for copy, _, receives in ships[name]:
            pl.when(receives)(copy.wait_recv)

    def sent(name):
        for copy, sends, _ in ships[name]:
            pl.when(sends)(copy.wait_send)

    @pl.when(jnp.logical_not(has_left))
    def _():
        in_l[...] = jnp.zeros_like(in_l)
        v0[1:3] = jnp.zeros_like(v0[1:3])
        scr[0:2] = jnp.zeros_like(scr[0:2])

    @pl.when(jnp.logical_not(has_right))
    def _():
        in_r[...] = jnp.zeros_like(in_r)
        v0[5:7] = jnp.zeros_like(v0[5:7])
        scr[4:6] = jnp.zeros_like(scr[4:6])

    @pl.when(me < 2)
    def _():
        v0[0] = jnp.zeros_like(v0[0])

    @pl.when(me >= n - 2)
    def _():
        v0[7] = jnp.zeros_like(v0[7])

    @pl.loop(0, chunks)
    def _(k):
        for copy in loads(k):
            copy.wait()

        @pl.when(k == chunks // 2)
        def _():
            scr_copy.wait()
            pl.semaphore_wait(barrier, n - 1)
            begin("screen")

        @pl.loop(0, CHUNK // 16)
        def _(j):
            start = pl.multiple_of(k * CHUNK + j * 16, 16)
            rows = pl.ds(start, 16)

            for c in range(3):
                for half in range(2):
                    low = gather_moments(pos, nrm, cnt, c, rows, half, 0, slots)
                    high = gather_moments(pos, nrm, cnt, c, rows, half, 1, slots)
                    own = pl.ds(pl.multiple_of(start + 8 * half, 8), 8)
                    for q in range(3):
                        planes = [[], [], [], []]
                        for r in range(3):
                            at = 3 * q + r
                            a = taps(low[at], low[9 + at], low[18 + at])
                            b = taps(high[at], high[9 + at], high[18 + at])
                            planes[0].append(a[0])
                            planes[1].append(a[1] + b[0])
                            planes[2].append(a[2] + b[1])
                            planes[3].append(b[2])
                        for i in range(4):
                            t = taps(*planes[i])
                            g[c, i, q, own, :] = lane_after(t[0]) + t[1] + lane_before(t[2])

    def along_y(c, i):
        t = taps(g[c, i, 0], g[c, i, 1], g[c, i, 2])
        return row_after(t[0]) + t[1] + row_before(t[2])

    def across(i):
        fy = along_y(1, i)
        fz = along_y(2, i)
        return (row_after(fy) - row_before(fy)) + (lane_after(fz) - lane_before(fz))

    scale = 1.0 / 16.0
    f0[0] = along_y(0, 0)
    f0[3] = along_y(0, 3)
    out_l[0] = scale * f0[0]
    out_r[1] = -scale * f0[3]
    begin("outer")
    f0[1] = along_y(0, 1)
    f0[2] = along_y(0, 2)
    out_l[1] = scale * (f0[1] + across(0))
    out_r[0] = scale * (across(3) - f0[2])
    begin("inner")
    inner0 = scale * (across(1) + f0[2] - jnp.where(has_left, f0[0], 0.0))
    v0[3] = inner0
    inner1 = scale * (across(2) + jnp.where(has_right, f0[3], 0.0) - f0[1])
    v0[4] = inner1
    arrive("outer")
    arrive("inner")
    v0[3] = v0[3] + (in_l[0] + in_r[0])
    v0[4] = v0[4] + (in_l[1] + in_r[1])
    for name in ("first", "second", "third"):
        begin(name)

    def smooth(a):
        a = row_before(a) + (a + a) + row_after(a)
        return lane_before(a) + (a + a) + lane_after(a)

    def apply(src, dst, smoothed, i, lo):
        u = smoothed[i] + (smoothed[i + 1] + smoothed[i + 1]) + smoothed[i + 2]
        out = (scr[lo + i] + (4.0 - SHIFT)) * src[i + 1] - scale * u
        if lo + i < 2:
            out = jnp.where(has_left, out, 0.0)
        if lo + i > 3:
            out = jnp.where(has_right, out, 0.0)
        dst[i] = out

    def dot(a, i, b, j):
        return jnp.sum(a[i] * b[j] + a[i + 1] * b[j + 1], axis=0, keepdims=True)

    def smooth_into(dst, src, planes):
        for i in planes:
            dst[i] = smooth(src[i])

    s0 = [g.at[0, i // 3, i % 3] for i in range(8)]
    s1 = [g.at[1, i // 3, i % 3] for i in range(6)]
    s2 = [g.at[2, i // 3, i % 3] for i in range(4)]

    class Planes:
        def __init__(self, refs):
            self.refs = refs

        def __getitem__(self, i):
            return self.refs[i][...]

        def __setitem__(self, i, value):
            self.refs[i][...] = value

    s0, s1, s2 = Planes(s0), Planes(s1), Planes(s2)
    smooth_into(s0, v0, (3, 4))
    part[0:1, :] = dot(v0, 3, v0, 3)
    arrive("screen")
    arrive("first")
    smooth_into(s0, v0, (2, 5))
    for i in (2, 3):
        apply(v0, v1, s0, i, 0)
    part[1:2, :] = dot(v0, 3, v1, 2)
    part[2:3, :] = dot(v1, 2, v1, 2)
    smooth_into(s1, v1, (2, 3))
    arrive("second")
    smooth_into(s0, v0, (1, 6))
    for i in (1, 4):
        apply(v0, v1, s0, i, 0)
    smooth_into(s1, v1, (1, 4))
    for i in (1, 2):
        apply(v1, v2, s1, i, 1)
    part[3:4, :] = dot(v1, 2, v2, 1)
    part[4:5, :] = dot(v2, 1, v2, 1)
    smooth_into(s2, v2, (1, 2))
    arrive("third")
    smooth_into(s0, v0, (0, 7))
    for i in (0, 5):
        apply(v0, v1, s0, i, 0)
    smooth_into(s1, v1, (0, 5))
    for i in (0, 3):
        apply(v1, v2, s1, i, 1)
    smooth_into(s2, v2, (0, 3))
    for i in (0, 1):
        apply(v2, v3, s2, i, 2)
    part[5:6, :] = dot(v2, 1, v3, 0)
    part[6:8, :] = jnp.zeros((2, part.shape[1]), jnp.float32)

    def spread(d):
        return pltpu.make_async_remote_copy(
            src_ref=part, dst_ref=parts.at[d], send_sem=psend.at[d], recv_sem=precv.at[d],
            device_id=peer(lax.rem(me + d, n)), device_id_type=MESH)

    @pl.loop(1, n)
    def _(d):
        spread(d).start()

    @pl.loop(1, n)
    def _(d):
        spread(d).wait_recv()

    def order(d, total):
        return total + parts[d]

    parts[0] = part[...]
    total = lax.fori_loop(0, n, order, jnp.zeros(part.shape, jnp.float32))
    total = jnp.sum(total, axis=1, keepdims=True)
    moment = [jnp.broadcast_to(total[k:k + 1, :], (8, 128)) for k in range(6)]

    def inner(a, b):
        terms = {}
        for i, s in enumerate(a):
            for j, t in enumerate(b):
                terms[i + j] = s * t if i + j not in terms else terms[i + j] + s * t
        out = None
        for k, s in terms.items():
            out = s * moment[k] if out is None else out + s * moment[k]
        return out

    one = jnp.ones((8, 128), jnp.float32)
    none = jnp.zeros((8, 128), jnp.float32)
    sol, res, way, rr = [], [one], [one], moment[0]
    for step in range(ITERS):
        image = [SHIFT * s for s in way] + [none]
        image = [image[k] + (way[k - 1] if k else none) for k in range(len(image))]
        alpha = rr / inner(way, image)
        sol = [(sol[k] if k < len(sol) else none) + alpha * s for k, s in enumerate(way)]
        res = [(res[k] if k < len(res) else none) - alpha * s for k, s in enumerate(image)]
        if step < ITERS - 1:
            new = inner(res, res)
            beta = new / rr
            way = [s + (beta * way[k] if k < len(way) else none) for k, s in enumerate(res)]
            rr = new

    sol = [s[0:1, :] for s in sol]
    res = [s[0:1, :] for s in res]
    for i in range(2):
        sol_ref[i] = sol[0] * v0[3 + i] + sol[1] * v1[2 + i] + sol[2] * v2[1 + i]
        res_ref[i] = res[0] * v0[3 + i] + res[1] * v1[2 + i] + res[2] * v2[1 + i] + res[3] * v3[i]

    @pl.loop(1, n)
    def _(d):
        spread(d).wait_send()

    for name in ships:
        sent(name)


def local(n, positions, normals, counts, screen):
    slots = positions.shape[1]
    plane = counts.shape[1:]
    chunks = plane[0] // CHUNK
    f32 = jnp.float32
    out = jax.ShapeDtypeStruct(counts.shape, f32)
    return tuple(pl.pallas_call(
        functools.partial(kernel, n, slots),
        out_shape=(out, out),
        in_specs=[pl.BlockSpec(memory_space=pl.ANY)] * 4,
        out_specs=(pl.BlockSpec(memory_space=pltpu.VMEM),) * 2,
        scratch_shapes=[
            pltpu.VMEM(positions.shape, positions.dtype),
            pltpu.VMEM(normals.shape, normals.dtype),
            pltpu.VMEM(counts.shape, counts.dtype),
            pltpu.VMEM((6,) + plane, f32),
            pltpu.VMEM((3, 4, 3) + plane, f32),
            pltpu.VMEM((4,) + plane, f32),
            pltpu.VMEM((2,) + plane, f32),
            pltpu.VMEM((2,) + plane, f32),
            pltpu.VMEM((2,) + plane, f32),
            pltpu.VMEM((2,) + plane, f32),
            pltpu.VMEM((8,) + plane, f32),
            pltpu.VMEM((6,) + plane, f32),
            pltpu.VMEM((4,) + plane, f32),
            pltpu.VMEM((2,) + plane, f32),
            pltpu.VMEM((8, 128), f32),
            pltpu.VMEM((n, 8, 128), f32),
            pltpu.SemaphoreType.DMA((4, chunks)),
            pltpu.SemaphoreType.DMA((12,)),
            pltpu.SemaphoreType.DMA((12,)),
            pltpu.SemaphoreType.DMA((n,)),
            pltpu.SemaphoreType.DMA((n,)),
        ],
        compiler_params=pltpu.CompilerParams(
            collective_id=0, has_side_effects=True, vmem_limit_bytes=60 * 1024 * 1024
        ),
    )(positions, normals, counts, screen))


def solution(mesh):
    placed = (
        P(None, None, "gx", "parts", None),
        P(None, None, "gx", "parts", None),
        P("gx", "parts", None),
        P("gx", "parts", None),
    )
    return jax.shard_map(
        functools.partial(local, mesh.shape["gx"]),
        mesh=mesh,
        in_specs=placed,
        out_specs=(P("gx", "parts", None), P("gx", "parts", None)),
        check_vma=False,
    )
```

```python
import functools

import jax
import jax.numpy as jnp
from jax import lax
from jax.experimental import pallas as pl
from jax.experimental.pallas import tpu as pltpu
from jax.sharding import PartitionSpec as P

ITERS = 3
SHIFT = 2.25
CHUNK = 32
MESH = pl.DeviceIdType.MESH


def lane_before(a):
    lane = lax.broadcasted_iota(jnp.int32, a.shape, 1)
    return jnp.where(lane == 0, 0.0, pltpu.roll(a, 1, 1))


def lane_after(a):
    lane = lax.broadcasted_iota(jnp.int32, a.shape, 1)
    size = a.shape[1]
    return jnp.where(lane == size - 1, 0.0, pltpu.roll(a, size - 1, 1))


def row_before(a):
    row = lax.broadcasted_iota(jnp.int32, a.shape, 0)
    return jnp.where(row == 0, 0.0, pltpu.roll(a, 1, 0))


def row_after(a):
    row = lax.broadcasted_iota(jnp.int32, a.shape, 0)
    size = a.shape[0]
    return jnp.where(row == size - 1, 0.0, pltpu.roll(a, size - 1, 0))


def taps(m0, m1, m2):
    last = m1 - m2
    return (m0 - m1) - m2, m0 + (m2 + m2), last


def gather_moments(pos, nrm, cnt, c, rows, half, plane, slots):
    part = slice(8 * half, 8 * half + 8)
    live = cnt[plane, rows, :][part]
    sums = [None] * 27
    for s in range(slots):
        n = nrm[c, s, plane, rows, :].astype(jnp.float32)[part]
        x = pos[0, s, plane, rows, :].astype(jnp.float32)[part]
        y = pos[1, s, plane, rows, :].astype(jnp.float32)[part]
        z = pos[2, s, plane, rows, :].astype(jnp.float32)[part]
        tx = jnp.where(live > s, n, 0.0)
        for p in range(3):
            if p:
                tx = tx * (x if p == 1 else 1.0 - x)
            ty = tx
            for q in range(3):
                if q:
                    ty = ty * (y if q == 1 else 1.0 - y)
                tz = ty
                for r in range(3):
                    if r:
                        tz = tz * (z if r == 1 else 1.0 - z)
                    at = 9 * p + 3 * q + r
                    sums[at] = tz if sums[at] is None else sums[at] + tz
    return sums


def kernel(n, slots, pos_hbm, nrm_hbm, cnt_hbm, scr_hbm, sol_ref, res_ref,
           pos, nrm, cnt, scr, g, f0, out_l, out_r, in_l, in_r, v0, v1, v2, v3, part, parts,
           load_sem, send_sem, recv_sem, psend, precv):
    me = lax.axis_index("gx")
    my_part = lax.axis_index("parts")
    ny = cnt.shape[1]
    chunks = ny // CHUNK
    has_left, has_right = me > 0, me < n - 1

    def peer(i):
        return {"parts": my_part, "gx": i}

    def loads(k):
        rows = pl.ds(pl.multiple_of(k * CHUNK, CHUNK), CHUNK)
        return (
            pltpu.make_async_copy(pos_hbm.at[:, :, :, rows, :], pos.at[:, :, :, rows, :], load_sem.at[0, k]),
            pltpu.make_async_copy(nrm_hbm.at[:, :, :, rows, :], nrm.at[:, :, :, rows, :], load_sem.at[1, k]),
            pltpu.make_async_copy(cnt_hbm.at[:, rows, :], cnt.at[:, rows, :], load_sem.at[2, k]),
        )

    for k in range(chunks):
        for copy in loads(k):
            copy.start()
    scr_copy = pltpu.make_async_copy(scr_hbm, scr.at[2:4], load_sem.at[3, 0])
    scr_copy.start()

    barrier = pltpu.get_barrier_semaphore()

    @pl.loop(1, n)
    def _(d):
        pl.semaphore_signal(barrier, inc=1, device_id=peer(lax.rem(me + d, n)), device_id_type=MESH)

    def ship(src, dst, by, at):
        copy = pltpu.make_async_remote_copy(
            src_ref=src, dst_ref=dst, send_sem=send_sem.at[at], recv_sem=recv_sem.at[at],
            device_id=peer(jnp.clip(me + by, 0, n - 1)), device_id_type=MESH)
        to, source = me + by, me - by
        return copy, (to >= 0) & (to < n), (source >= 0) & (source < n)

    ships = {
        "screen": (ship(scr.at[2:4], scr.at[4:6], -1, 0), ship(scr.at[2:4], scr.at[0:2], 1, 1)),
        "outer": (ship(out_l.at[0], in_r.at[0], -1, 2), ship(out_r.at[1], in_l.at[1], 1, 3)),
        "inner": (ship(out_l.at[1], in_r.at[1], -1, 10), ship(out_r.at[0], in_l.at[0], 1, 11)),
        "first": (ship(v0.at[3], v0.at[5], -1, 4), ship(v0.at[4], v0.at[2], 1, 5)),
        "second": (ship(v0.at[4], v0.at[6], -1, 6), ship(v0.at[3], v0.at[1], 1, 7)),
        "third": (ship(v0.at[3], v0.at[7], -2, 8),),
        "last": (ship(v0.at[4], v0.at[0], 2, 9),),
    }

    def begin(name):
        for copy, sends, _ in ships[name]:
            pl.when(sends)(copy.start)

    def arrive(name):
        for copy, _, receives in ships[name]:
            pl.when(receives)(copy.wait_recv)

    def sent(name):
        for copy, sends, _ in ships[name]:
            pl.when(sends)(copy.wait_send)

    @pl.when(jnp.logical_not(has_left))
    def _():
        in_l[...] = jnp.zeros_like(in_l)
        v0[1:3] = jnp.zeros_like(v0[1:3])
        scr[0:2] = jnp.zeros_like(scr[0:2])

    @pl.when(jnp.logical_not(has_right))
    def _():
        in_r[...] = jnp.zeros_like(in_r)
        v0[5:7] = jnp.zeros_like(v0[5:7])
        scr[4:6] = jnp.zeros_like(scr[4:6])

    @pl.when(me < 2)
    def _():
        v0[0] = jnp.zeros_like(v0[0])

    @pl.when(me >= n - 2)
    def _():
        v0[7] = jnp.zeros_like(v0[7])

    @pl.loop(0, chunks)
    def _(k):
        for copy in loads(k):
            copy.wait()

        @pl.when(k == chunks // 2)
        def _():
            scr_copy.wait()
            pl.semaphore_wait(barrier, n - 1)
            begin("screen")

        @pl.loop(0, CHUNK // 16)
        def _(j):
            start = pl.multiple_of(k * CHUNK + j * 16, 16)
            rows = pl.ds(start, 16)

            for c in range(3):
                for half in range(2):
                    low = gather_moments(pos, nrm, cnt, c, rows, half, 0, slots)
                    high = gather_moments(pos, nrm, cnt, c, rows, half, 1, slots)
                    own = pl.ds(pl.multiple_of(start + 8 * half, 8), 8)
                    for q in range(3):
                        planes = [[], [], [], []]
                        for r in range(3):
                            at = 3 * q + r
                            a = taps(low[at], low[9 + at], low[18 + at])
                            b = taps(high[at], high[9 + at], high[18 + at])
                            planes[0].append(a[0])
                            planes[1].append(a[1] + b[0])
                            planes[2].append(a[2] + b[1])
                            planes[3].append(b[2])
                        for i in range(4):
                            t = taps(*planes[i])
                            g[c, i, q, own, :] = lane_after(t[0]) + t[1] + lane_before(t[2])

    def along_y(c, i):
        t = taps(g[c, i, 0], g[c, i, 1], g[c, i, 2])
        return row_after(t[0]) + t[1] + row_before(t[2])

    def across(i):
        fy = along_y(1, i)
        fz = along_y(2, i)
        return (row_after(fy) - row_before(fy)) + (lane_after(fz) - lane_before(fz))

    scale = 1.0 / 16.0
    f0[0] = along_y(0, 0)
    f0[3] = along_y(0, 3)
    out_l[0] = scale * f0[0]
    out_r[1] = -scale * f0[3]
    begin("outer")
    f0[1] = along_y(0, 1)
    f0[2] = along_y(0, 2)
    out_l[1] = scale * (f0[1] + across(0))
    out_r[0] = scale * (across(3) - f0[2])
    begin("inner")
    inner0 = scale * (across(1) + f0[2] - jnp.where(has_left, f0[0], 0.0))
    v0[3] = inner0
    inner1 = scale * (across(2) + jnp.where(has_right, f0[3], 0.0) - f0[1])
    v0[4] = inner1
    arrive("outer")
    arrive("inner")
    v0[3] = v0[3] + (in_l[0] + in_r[0])
    v0[4] = v0[4] + (in_l[1] + in_r[1])
    for name in ("first", "second", "third"):
        begin(name)

    def smooth(a):
        a = row_before(a) + (a + a) + row_after(a)
        return lane_before(a) + (a + a) + lane_after(a)

    def apply(src, dst, smoothed, i, lo):
        u = smoothed[i] + (smoothed[i + 1] + smoothed[i + 1]) + smoothed[i + 2]
        out = (scr[lo + i] + (4.0 - SHIFT)) * src[i + 1] - scale * u
        if lo + i < 2:
            out = jnp.where(has_left, out, 0.0)
        if lo + i > 3:
            out = jnp.where(has_right, out, 0.0)
        dst[i] = out

    def dot(a, i, b, j):
        return jnp.sum(a[i] * b[j] + a[i + 1] * b[j + 1], axis=0, keepdims=True)

    def smooth_into(dst, src, planes):
        for i in planes:
            dst[i] = smooth(src[i])

    s0 = [g.at[0, i // 3, i % 3] for i in range(8)]
    s1 = [g.at[1, i // 3, i % 3] for i in range(6)]
    s2 = [g.at[2, i // 3, i % 3] for i in range(4)]

    class Planes:
        def __init__(self, refs):
            self.refs = refs

        def __getitem__(self, i):
            return self.refs[i][...]

        def __setitem__(self, i, value):
            self.refs[i][...] = value

    s0, s1, s2 = Planes(s0), Planes(s1), Planes(s2)
    smooth_into(s0, v0, (3, 4))
    part[0:1, :] = dot(v0, 3, v0, 3)
    arrive("screen")
    arrive("first")
    smooth_into(s0, v0, (2, 5))
    for i in (2, 3):
        apply(v0, v1, s0, i, 0)
    part[1:2, :] = dot(v0, 3, v1, 2)
    part[2:3, :] = dot(v1, 2, v1, 2)
    smooth_into(s1, v1, (2, 3))
    arrive("second")
    smooth_into(s0, v0, (1, 6))
    for i in (1, 4):
        apply(v0, v1, s0, i, 0)
    smooth_into(s1, v1, (1, 4))
    for i in (1, 2):
        apply(v1, v2, s1, i, 1)
    part[3:4, :] = dot(v1, 2, v2, 1)
    part[4:5, :] = dot(v2, 1, v2, 1)
    smooth_into(s2, v2, (1, 2))
    arrive("third")
    smooth_into(s0, v0, (7,))
    apply(v0, v1, s0, 5, 0)
    smooth_into(s1, v1, (5,))
    apply(v1, v2, s1, 3, 1)
    smooth_into(s2, v2, (3,))
    terms = [
        v2[i] * ((scr[i + 1] + (4.0 - SHIFT)) * v2[i] - (2.0 * scale) * (s2[i] + s2[i + 1]))
        for i in (1, 2)
    ]
    part[5:6, :] = jnp.sum(terms[0] + terms[1], axis=0, keepdims=True)
    part[6:8, :] = jnp.zeros((2, part.shape[1]), jnp.float32)

    def spread(d):
        return pltpu.make_async_remote_copy(
            src_ref=part, dst_ref=parts.at[d], send_sem=psend.at[d], recv_sem=precv.at[d],
            device_id=peer(lax.rem(me + d, n)), device_id_type=MESH)

    @pl.loop(1, n)
    def _(d):
        spread(d).start()

    begin("last")
    arrive("last")
    smooth_into(s0, v0, (0,))
    apply(v0, v1, s0, 0, 0)
    smooth_into(s1, v1, (0,))
    apply(v1, v2, s1, 0, 1)
    smooth_into(s2, v2, (0,))
    for i in (0, 1):
        apply(v2, v3, s2, i, 2)

    @pl.loop(1, n)
    def _(d):
        spread(d).wait_recv()

    def order(d, total):
        return total + parts[d]

    parts[0] = part[...]
    total = lax.fori_loop(0, n, order, jnp.zeros(part.shape, jnp.float32))
    total = jnp.sum(total, axis=1, keepdims=True)
    moment = [jnp.broadcast_to(total[k:k + 1, :], (8, 128)) for k in range(6)]

    def inner(a, b):
        terms = {}
        for i, s in enumerate(a):
            for j, t in enumerate(b):
                terms[i + j] = s * t if i + j not in terms else terms[i + j] + s * t
        out = None
        for k, s in terms.items():
            out = s * moment[k] if out is None else out + s * moment[k]
        return out

    one = jnp.ones((8, 128), jnp.float32)
    none = jnp.zeros((8, 128), jnp.float32)
    sol, res, way, rr = [], [one], [one], moment[0]
    for step in range(ITERS):
        image = [SHIFT * s for s in way] + [none]
        image = [image[k] + (way[k - 1] if k else none) for k in range(len(image))]
        alpha = rr / inner(way, image)
        sol = [(sol[k] if k < len(sol) else none) + alpha * s for k, s in enumerate(way)]
        res = [(res[k] if k < len(res) else none) - alpha * s for k, s in enumerate(image)]
        if step < ITERS - 1:
            new = inner(res, res)
            beta = new / rr
            way = [s + (beta * way[k] if k < len(way) else none) for k, s in enumerate(res)]
            rr = new

    sol = [s[0:1, :] for s in sol]
    res = [s[0:1, :] for s in res]
    for i in range(2):
        sol_ref[i] = sol[0] * v0[3 + i] + sol[1] * v1[2 + i] + sol[2] * v2[1 + i]
        res_ref[i] = res[0] * v0[3 + i] + res[1] * v1[2 + i] + res[2] * v2[1 + i] + res[3] * v3[i]

    @pl.loop(1, n)
    def _(d):
        spread(d).wait_send()

    for name in ships:
        sent(name)


def local(n, positions, normals, counts, screen):
    slots = positions.shape[1]
    plane = counts.shape[1:]
    chunks = plane[0] // CHUNK
    f32 = jnp.float32
    out = jax.ShapeDtypeStruct(counts.shape, f32)
    return tuple(pl.pallas_call(
        functools.partial(kernel, n, slots),
        out_shape=(out, out),
        in_specs=[pl.BlockSpec(memory_space=pl.ANY)] * 4,
        out_specs=(pl.BlockSpec(memory_space=pltpu.VMEM),) * 2,
        scratch_shapes=[
            pltpu.VMEM(positions.shape, positions.dtype),
            pltpu.VMEM(normals.shape, normals.dtype),
            pltpu.VMEM(counts.shape, counts.dtype),
            pltpu.VMEM((6,) + plane, f32),
            pltpu.VMEM((3, 4, 3) + plane, f32),
            pltpu.VMEM((4,) + plane, f32),
            pltpu.VMEM((2,) + plane, f32),
            pltpu.VMEM((2,) + plane, f32),
            pltpu.VMEM((2,) + plane, f32),
            pltpu.VMEM((2,) + plane, f32),
            pltpu.VMEM((8,) + plane, f32),
            pltpu.VMEM((6,) + plane, f32),
            pltpu.VMEM((4,) + plane, f32),
            pltpu.VMEM((2,) + plane, f32),
            pltpu.VMEM((8, 128), f32),
            pltpu.VMEM((n, 8, 128), f32),
            pltpu.SemaphoreType.DMA((4, chunks)),
            pltpu.SemaphoreType.DMA((12,)),
            pltpu.SemaphoreType.DMA((12,)),
            pltpu.SemaphoreType.DMA((n,)),
            pltpu.SemaphoreType.DMA((n,)),
        ],
        compiler_params=pltpu.CompilerParams(
            collective_id=0, has_side_effects=True, vmem_limit_bytes=60 * 1024 * 1024
        ),
    )(positions, normals, counts, screen))


def solution(mesh):
    placed = (
        P(None, None, "gx", "parts", None),
        P(None, None, "gx", "parts", None),
        P("gx", "parts", None),
        P("gx", "parts", None),
    )
    return jax.shard_map(
        functools.partial(local, mesh.shape["gx"]),
        mesh=mesh,
        in_specs=placed,
        out_specs=(P("gx", "parts", None), P("gx", "parts", None)),
        check_vma=False,
    )
```
